32 devices in a mesh: dp: 4 (over z), mp: 8 (over y, x, core).
Axes of the slice: x: 2, y: 2, z: 4, core: 2. Of those that a mesh axis runs over, the one named last changes fastest.
Arguments:
- activations: bfloat16 [8192, 8192], P('dp', 'mp'), as said below
- output_grads: bfloat16 [8192, 28672], P('dp', 'mp'), as said below
- probe_matrix: bfloat16 [28672, 128], P('mp'), may hold values from -6 to 6
Outputs:
- basis: float32 [8192, 128], P('mp')
- projection: float32 [128, 28672], P(None, 'mp')
The draws below stay inside these ranges and needn't reach their ends.
Inputs may be any that keep to these rules, and one draw needn't show every extreme that they name: `activations`: finite real values of order one. `output_grads`: finite real values of order one.
All inputs are finite; a program needn't handle non-finite values.
Results may differ from the reference program's by a relative error of at most 0.035.
Values may be sent and summed in bfloat16 or wider, within the bound.
A program may use at most 64 MiB of HBM per device.

```python
import jax
import jax.numpy as jnp
from jax import lax

H = 8192
F = 28672
K = 128
TOKENS = 8192
N_MP = 8


def column_scales(key, width, blocks, spread):
    position = jnp.arange(width, dtype=jnp.float32)
    span = width // blocks
    inner = (jnp.arange(width) % span).astype(jnp.float32) / span
    rough = jax.random.uniform(key, (width,), jnp.float32, 0.7, 1.4)
    return jnp.exp(jnp.log(spread) * (position + 0.5) / width + jnp.log(3.0) * inner) * rough


def scaled_field(key, rows, width, blocks):
    first_key, second_key = jax.random.split(key, 2)
    spread = 30.0
    noise = jnp.clip(jax.random.normal(first_key, (rows, width), jnp.float32), -6.0, 6.0)
    scales = column_scales(second_key, width, blocks, spread)
    scales = scales / jnp.sqrt(jnp.mean(scales * scales))
    return noise * scales


def draw_activations(key, part):
    field = scaled_field(jax.random.fold_in(key, 11), TOKENS, H, N_MP)
    return (field / jnp.sqrt(jnp.float32(TOKENS))).astype(jnp.bfloat16)


def draw_output_grads(key, part):
    field = scaled_field(jax.random.fold_in(key, 23), TOKENS, F, N_MP)
    return field.astype(jnp.bfloat16)


def shard_levels(rng, dims, shards, least, high):
    factor_of, own = 1.0, jax.random.fold_in(rng, 6)
    for dim, blocks in shards:
        heights = jnp.exp(jax.random.uniform(jax.random.fold_in(own, dim), (blocks,), jnp.float32, least / len(shards), high / len(shards)))
        factor_of = factor_of * jnp.repeat(heights, dims[dim] // blocks).reshape([-1 if axis == dim else 1 for axis in range(len(dims))])
    return factor_of


def scatter_about(key, dims, deviation, most, cuts=(), held_as=jnp.bfloat16):
    values = jax.random.normal(key, dims, jnp.float32) * deviation
    if len(cuts) > 0:
        values = shard_levels(key, dims, cuts, -0.22, 0.18) * values
    return jnp.clip(values, min=-most, max=most).astype(held_as)


def setup_inputs(seed: int = 0) -> dict:
    seeds = jax.random.split(jax.random.key(seed), 4)
    activations = draw_activations(jax.random.fold_in(seeds[3], 71), 0)
    output_grads = draw_output_grads(jax.random.fold_in(seeds[3], 71), 0)
    probe_matrix = scatter_about(seeds[2], (F, K), 1.0, 6.0, ((0, 8),))
    return {"activations": activations, "output_grads": output_grads, "probe_matrix": probe_matrix}


def contract_rows(left, right):
    return lax.dot_general(left.astype(jnp.float32), right.astype(jnp.float32), (((0,), (0,)), ((), ())), preferred_element_type=jnp.float32)

def blocked_total(left, right):
    span = left.shape[1] // N_MP

    def add_block(index, total):
        start = (index * span).astype(jnp.int32)
        columns = lax.dynamic_slice_in_dim(left, start, span, 1)
        pieces = lax.dynamic_slice_in_dim(right, start, span, 0)
        term = jnp.dot(columns.astype(jnp.float32), pieces.astype(jnp.float32), preferred_element_type=jnp.float32)
        term = lax.optimization_barrier(term.astype(jnp.bfloat16)).astype(jnp.float32)
        return total + term
    start_total = jnp.zeros((left.shape[0], right.shape[1]), jnp.float32)
    return lax.fori_loop(0, N_MP, add_block, start_total).astype(jnp.bfloat16)

def orthonormalize(matrix):
    gram_matrix = lax.dot_general(matrix.astype(jnp.float32), matrix.astype(jnp.float32), (((0,), (0,)), ((), ())), precision=lax.Precision.HIGHEST, preferred_element_type=jnp.float32)
    factor = jnp.linalg.cholesky(gram_matrix)
    return lax.linalg.triangular_solve(factor, matrix, left_side=False, lower=True, transpose_a=True)

def reference(activations, output_grads, probe_matrix):
    probe_rows = blocked_total(output_grads, probe_matrix)
    first_basis = orthonormalize(contract_rows(activations, probe_rows))
    token_rows = blocked_total(activations, first_basis.astype(jnp.bfloat16))
    second_basis = orthonormalize(contract_rows(output_grads, token_rows))
    unit_rows = blocked_total(output_grads, second_basis.astype(jnp.bfloat16))
    third_basis = orthonormalize(contract_rows(activations, unit_rows))
    last_rows = blocked_total(activations, third_basis.astype(jnp.bfloat16))
    projection = contract_rows(last_rows, output_grads)
    basis = third_basis * jnp.sqrt(jnp.float32(H))
    return (basis, projection)
```

```python
import functools

import jax
import jax.numpy as jnp
from jax import lax
from jax.experimental import pallas as pl
from jax.experimental.pallas import tpu as pltpu
from jax.sharding import PartitionSpec as P

H = 8192
F32, BF16 = jnp.float32, jnp.bfloat16
MESH = pl.DeviceIdType.MESH


def inverse_factor(gram):
    k = gram.shape[0]
    row_id = lax.broadcasted_iota(jnp.int32, (k, k), 0)
    lane_id = lax.broadcasted_iota(jnp.int32, (k, k), 1)
    row_of = lax.broadcasted_iota(jnp.int32, (k, 1), 0)
    eye = row_id == lane_id

    def step(j, carry):
        m, e = carry
        col = jnp.sum(jnp.where(lane_id == j, m, 0.0), axis=1, keepdims=True)
        row = jnp.sum(jnp.where(row_id == j, m, 0.0), axis=0, keepdims=True)
        done = jnp.sum(jnp.where(row_id == j, e, 0.0), axis=0, keepdims=True)
        pivot = jnp.sum(jnp.where(row_of == j, col, 0.0), axis=0, keepdims=True)
        scale = jnp.where(row_of > j, col * (1.0 / pivot), 0.0)
        return m - scale * row, e - scale * done

    m, e = lax.fori_loop(0, k, step, (gram, jnp.where(eye, 1.0, 0.0).astype(F32)))
    pivots = jnp.sum(jnp.where(eye, m, 0.0), axis=1, keepdims=True)
    return e * lax.rsqrt(pivots)


def kernel(
    n_dp, n_mp, acts, grads, probe, basis_t, proj,
    acts_v, grads_v, probe_v,
    part0, part1, part2, part3, came0, came1, came2, came3, rows0, rows1, rows2, rows3,
    sent0, sent1, sent2, sent3, got0, got1, got2, got3, sk0, sk1, sk2,
    gram_part, gram_came, gram_all, factor,
    load_sem, mp_send, mp_recv, dp_send, dp_recv, g_send, g_recv,
):
    me_d, me_m = lax.axis_index("dp"), lax.axis_index("mp")
    tokens, k = acts_v.shape[0], probe_v.shape[1]
    span = tokens // n_mp
    parts, cames = (part0, part1, part2, part3), (came0, came1, came2, came3)
    rows = (rows0, rows1, rows2, rows3)
    sents, gots = (sent0, sent1, sent2, sent3), (got0, got1, got2, got3)
    sketches = (sk0, sk1, sk2, proj)

    def span_of(c):
        return pl.ds(pl.multiple_of(c * span, span), span)

    def grads_load(c):
        return pltpu.make_async_copy(
            grads.at[span_of(c), :], grads_v.at[span_of(c), :], load_sem.at[c]
        )

    probe_load = pltpu.make_async_copy(probe, probe_v, load_sem.at[n_mp])
    acts_load = pltpu.make_async_copy(acts, acts_v, load_sem.at[n_mp + 1])
    probe_load.start()
    for i in range(n_mp):
        grads_load(lax.rem(me_m + 1 + i, n_mp)).start()
    acts_load.start()

    barrier = pltpu.get_barrier_semaphore()
    for i in range(1, n_mp):
        pl.semaphore_signal(
            barrier, inc=1, device_id={"mp": lax.rem(me_m + i, n_mp)}, device_id_type=MESH
        )
    for i in range(1, n_dp):
        pl.semaphore_signal(
            barrier, inc=1, device_id={"dp": lax.rem(me_d + i, n_dp)}, device_id_type=MESH
        )
    probe_load.wait()
    pl.semaphore_wait(barrier, n_mp + n_dp - 2)

    def copy(axis, src, dst, send, recv, peer):
        return pltpu.make_async_remote_copy(
            src_ref=src, dst_ref=dst, send_sem=send, recv_sem=recv,
            device_id={axis: peer}, device_id_type=MESH,
        )

    def gather_rows(s, piece):
        target = rows[s].at[:, span_of(me_m)]
        target[...] = piece.astype(BF16)

        def send(i, _):
            peer = lax.rem(me_m + i, n_mp)
            copy("mp", target, target, mp_send.at[s, 1, peer], mp_recv.at[s, 1, me_m], peer).start()
            return 0

        def wait(i, _):
            peer = lax.rem(me_m + i, n_mp)
            theirs = rows[s].at[:, span_of(peer)]
            copy("mp", target, theirs, mp_send.at[s, 1, peer], mp_recv.at[s, 1, peer], peer).wait()
            return 0

        lax.fori_loop(1, n_mp, send, 0)
        lax.fori_loop(1, n_mp, wait, 0)

    def scatter_rows(s, product, first, last):
        def body(i, _):
            c = lax.rem(me_m + i, n_mp)
            parts[s].at[c][...] = product(c).astype(BF16)

            @pl.when(i < n_mp)
            def _():
                copy(
                    "mp", parts[s].at[c], cames[s].at[me_m],
                    mp_send.at[s, 0, c], mp_recv.at[s, 0, me_m], c,
                ).start()

            return 0

        lax.fori_loop(first, last, body, 0)

    def collect_rows(s):
        def add(i, total):
            peer = lax.rem(me_m + i, n_mp)
            copy(
                "mp", parts[s].at[peer], cames[s].at[peer],
                mp_send.at[s, 0, peer], mp_recv.at[s, 0, peer], peer,
            ).wait()
            return total + cames[s].at[peer][...].astype(F32)

        return lax.fori_loop(1, n_mp, add, parts[s].at[me_m][...].astype(F32))

    def sum_tokens(s, field):
        width = field.shape[1] // n_dp

        def cols(j):
            return pl.ds(pl.multiple_of(j * width, 128), width)

        def body(i, _):
            j = lax.rem(me_d + i, n_dp)
            sents[s].at[j][...] = jnp.dot(
                rows[s][...], field[:, cols(j)], preferred_element_type=F32
            ).astype(BF16)

            @pl.when(i < n_dp)
            def _():
                copy(
                    "dp", sents[s].at[j], gots[s].at[me_d],
                    dp_send.at[s, 0, j], dp_recv.at[s, 0, me_d], j,
                ).start()

            return 0

        lax.fori_loop(1, n_dp + 1, body, 0)
        total = sents[s].at[me_d][...].astype(F32)
        for i in range(1, n_dp):
            peer = lax.rem(me_d + i, n_dp)
            copy(
                "dp", sents[s].at[peer], gots[s].at[peer],
                dp_send.at[s, 0, peer], dp_recv.at[s, 0, peer], peer,
            ).wait()
            total = total + gots[s].at[peer][...].astype(F32)
        target = sketches[s].at[:, cols(me_d)]
        target[...] = total.astype(BF16)
        for i in range(1, n_dp):
            peer = lax.rem(me_d + i, n_dp)
            copy("dp", target, target, dp_send.at[s, 1, peer], dp_recv.at[s, 1, me_d], peer).start()
        for i in range(1, n_dp):
            peer = lax.rem(me_d + i, n_dp)
            theirs = sketches[s].at[:, cols(peer)]
            copy("dp", target, theirs, dp_send.at[s, 1, peer], dp_recv.at[s, 1, peer], peer).wait()

    g_rows = k // n_mp

    def g_span(c):
        return pl.ds(pl.multiple_of(c * g_rows, g_rows), g_rows)

    def gram_start(s):
        sketch = sketches[s][...]
        gram_part.at[s][...] = lax.dot_general(
            sketch, sketch, (((1,), (1,)), ((), ())), preferred_element_type=F32
        )
        gram_came.at[s, me_m][...] = gram_part.at[s, g_span(me_m), :][...]
        for i in range(1, n_mp):
            peer = lax.rem(me_m + i, n_mp)
            copy(
                "mp", gram_part.at[s, g_span(peer), :], gram_came.at[s, me_m],
                g_send.at[s, 0, peer], g_recv.at[s, 0, me_m], peer,
            ).start()

    def gram_middle(s):
        for i in range(1, n_mp):
            peer = lax.rem(me_m + i, n_mp)
            copy(
                "mp", gram_part.at[s, g_span(peer), :], gram_came.at[s, peer],
                g_send.at[s, 0, peer], g_recv.at[s, 0, peer], peer,
            ).wait()
        target = gram_all.at[s, g_span(me_m), :]
        total = gram_came.at[s, 0][...]
        for i in range(1, n_mp):
            total = total + gram_came.at[s, i][...]
        target[...] = total
        for i in range(1, n_mp):
            peer = lax.rem(me_m + i, n_mp)
            copy("mp", target, target, g_send.at[s, 1, peer], g_recv.at[s, 1, me_m], peer).start()

    def gram_end(s):
        target = gram_all.at[s, g_span(me_m), :]
        for i in range(1, n_mp):
            peer = lax.rem(me_m + i, n_mp)
            theirs = gram_all.at[s, g_span(peer), :]
            copy("mp", target, theirs, g_send.at[s, 1, peer], g_recv.at[s, 1, peer], peer).wait()
        factor[...] = inverse_factor(gram_all.at[s][...])

    def probe_product(c):
        grads_load(c).wait()
        return jnp.dot(grads_v[span_of(c), :], probe_v[...], preferred_element_type=F32)

    scatter_rows(0, probe_product, 1, n_mp + 1)
    gather_rows(0, collect_rows(0).T)
    acts_load.wait()

    for s, (field, into) in enumerate(((acts_v, acts_v), (grads_v, grads_v), (acts_v, acts_v))):
        sum_tokens(s, field)
        gram_start(s)

        def product(c, s=s, into=into):
            return lax.dot_general(
                into[span_of(c), :], sketches[s][...],
                (((1,), (1,)), ((), ())), preferred_element_type=F32,
            )

        scatter_rows(s + 1, product, 1, n_mp // 2 + 1)
        gram_middle(s)
        scatter_rows(s + 1, product, n_mp // 2 + 1, n_mp + 1)
        gram_end(s)
        total = collect_rows(s + 1)
        gather_rows(
            s + 1,
            lax.dot_general(
                factor[...], total, (((1,), (1,)), ((), ())),
                precision=lax.Precision.HIGHEST, preferred_element_type=F32,
            ),
        )
    basis_t[...] = jnp.dot(
        factor[...], sk2[...].astype(F32),
        precision=lax.Precision.HIGHEST, preferred_element_type=F32,
    )
    sum_tokens(3, grads_v)


def fused(n_dp, n_mp, activations, output_grads, probe_matrix):
    tokens, features = activations.shape
    units, k = probe_matrix.shape
    span = tokens // n_mp
    widths = (features, units, features, units)
    any_space = pl.BlockSpec(memory_space=pl.ANY)
    vmem = pl.BlockSpec(memory_space=pltpu.VMEM)
    pieces = [pltpu.VMEM((n_mp, span, k), BF16)] * 4
    columns = [pltpu.VMEM((n_dp, k, w // n_dp), BF16) for w in widths]
    basis_t, proj = pl.pallas_call(
        functools.partial(kernel, n_dp, n_mp),
        out_shape=(
            jax.ShapeDtypeStruct((k, features), F32),
            jax.ShapeDtypeStruct((k, units), BF16),
        ),
        in_specs=[any_space] * 3,
        out_specs=(vmem, vmem),
        scratch_shapes=[
            pltpu.VMEM(activations.shape, BF16),
            pltpu.VMEM(output_grads.shape, BF16),
            pltpu.VMEM(probe_matrix.shape, BF16),
            *pieces,
            *pieces,
            *[pltpu.VMEM((k, tokens), BF16)] * 4,
            *columns,
            *columns,
            *[pltpu.VMEM((k, w), BF16) for w in widths[:3]],
            pltpu.VMEM((3, k, k), F32),
            pltpu.VMEM((3, n_mp, k // n_mp, k), F32),
            pltpu.VMEM((3, k, k), F32),
            pltpu.VMEM((k, k), F32),
            pltpu.SemaphoreType.DMA((n_mp + 2,)),
            pltpu.SemaphoreType.DMA((4, 2, n_mp)),
            pltpu.SemaphoreType.DMA((4, 2, n_mp)),
            pltpu.SemaphoreType.DMA((4, 2, n_dp)),
            pltpu.SemaphoreType.DMA((4, 2, n_dp)),
            pltpu.SemaphoreType.DMA((3, 2, n_mp)),
            pltpu.SemaphoreType.DMA((3, 2, n_mp)),
        ],
        compiler_params=pltpu.CompilerParams(
            collective_id=0, has_side_effects=True, vmem_limit_bytes=56 * 2**20
        ),
    )(activations, output_grads, probe_matrix)
    return (basis_t * jnp.sqrt(F32(H))).T, proj.astype(F32)


def contract_rows(left, right):
    return lax.dot_general(left, right, (((0,), (0,)), ((), ())), preferred_element_type=F32)


def token_total(partial_value):
    return lax.psum(partial_value.astype(BF16), "mp")


def orthonormalize(partial_value):
    summed = lax.psum(partial_value, "dp")
    gram = lax.dot_general(
        summed, summed, (((0,), (0,)), ((), ())),
        precision=lax.Precision.HIGHEST, preferred_element_type=F32,
    )
    factor = jnp.linalg.cholesky(lax.psum(gram, "mp"))
    return lax.linalg.triangular_solve(
        factor, summed, left_side=False, lower=True, transpose_a=True
    )


def separate(activations, output_grads, probe_matrix):
    def rows_of(field, columns):
        return token_total(jnp.dot(field, columns.astype(BF16), preferred_element_type=F32))

    first = orthonormalize(contract_rows(activations, rows_of(output_grads, probe_matrix)))
    second = orthonormalize(contract_rows(output_grads, rows_of(activations, first)))
    third = orthonormalize(contract_rows(activations, rows_of(output_grads, second)))
    projection = lax.psum(contract_rows(rows_of(activations, third), output_grads), "dp")
    return third * jnp.sqrt(F32(H)), projection


def solution(mesh):
    n_dp, n_mp = mesh.shape["dp"], mesh.shape["mp"]

    def on_device(activations, output_grads, probe_matrix):
        tokens, features = activations.shape
        units, k = probe_matrix.shape
        even = (
            features % (128 * n_dp) == 0
            and units % (128 * n_dp) == 0
            and tokens % (128 * n_mp) == 0
            and k % (8 * n_mp) == 0
        )
        run = functools.partial(fused, n_dp, n_mp) if even else separate
        return run(activations, output_grads, probe_matrix)

    in_specs = (P("dp", "mp"), P("dp", "mp"), P("mp", None))
    out_specs = (P("mp", None), P(None, "mp"))
    return jax.shard_map(
        on_device, mesh=mesh, in_specs=in_specs, out_specs=out_specs, check_vma=False
    )
```

```python
import functools

import jax
import jax.numpy as jnp
from jax import lax
from jax.experimental import pallas as pl
from jax.experimental.pallas import tpu as pltpu
from jax.sharding import PartitionSpec as P

H = 8192
F32, BF16 = jnp.float32, jnp.bfloat16
MESH = pl.DeviceIdType.MESH


def inverse_factor(gram):
    k = gram.shape[0]
    row_id = lax.broadcasted_iota(jnp.int32, (k, k), 0)
    lane_id = lax.broadcasted_iota(jnp.int32, (k, k), 1)
    lane_of = lax.broadcasted_iota(jnp.int32, (8, k), 1)
    row_of = lax.broadcasted_iota(jnp.int32, (k, 1), 0)
    group_id = lax.broadcasted_iota(jnp.int32, (k // 8, 8, k), 0)
    eye = row_id == lane_id

    def group_of(x, g):
        return jnp.sum(jnp.where(group_id == g, x.reshape(k // 8, 8, k), 0.0), axis=0)

    def lane_at(x, lanes, j):
        return jnp.sum(jnp.where(lanes == j, x, 0.0), axis=1, keepdims=True)

    def step(g, carry):
        m, e = carry
        for half in (0, 4):
            m_rows, e_rows = group_of(m, g), group_of(e, g)
            at = [8 * g + half + p for p in range(4)]
            cols = [lane_at(m, lane_id, j) for j in at]
            small = [lane_at(m_rows, lane_of, j) for j in at]
            rows = [m_rows[half + p : half + p + 1, :] for p in range(4)]
            done = [e_rows[half + p : half + p + 1, :] for p in range(4)]
            for p in range(4):
                inverse = 1.0 / small[p][half + p : half + p + 1, :]
                for q in range(p + 1, 4):
                    ratio = small[p][half + q : half + q + 1, :] * inverse
                    rows[q] = rows[q] - ratio * rows[p]
                    done[q] = done[q] - ratio * done[p]
                    cols[q] = cols[q] - ratio * cols[p]
                    small[q] = small[q] - ratio * small[p]
                scale = jnp.where(row_of > at[p], cols[p] * inverse, 0.0)
                m = m - scale * rows[p]
                e = e - scale * done[p]
        return m, e

    m, e = lax.fori_loop(0, k // 8, step, (gram, jnp.where(eye, 1.0, 0.0).astype(F32)))
    pivots = jnp.sum(jnp.where(eye, m, 0.0), axis=1, keepdims=True)
    return e * lax.rsqrt(pivots)


def kernel(
    n_dp, n_mp, acts, grads, probe, basis_t, proj,
    acts_v, grads_v, probe_v,
    part0, part1, part2, part3, came0, came1, came2, came3, rows0, rows1, rows2, rows3,
    sent0, sent1, sent2, sent3, got0, got1, got2, got3, sk0, sk1, sk2,
    gram_part, gram_came, gram_all, factor,
    load_sem, mp_send, mp_recv, dp_send, dp_recv, g_send, g_recv,
):
    me_d, me_m = lax.axis_index("dp"), lax.axis_index("mp")
    tokens, k = acts_v.shape[0], probe_v.shape[1]
    span = tokens // n_mp
    parts, cames = (part0, part1, part2, part3), (came0, came1, came2, came3)
    rows = (rows0, rows1, rows2, rows3)
    sents, gots = (sent0, sent1, sent2, sent3), (got0, got1, got2, got3)
    sketches = (sk0, sk1, sk2, proj)

    def span_of(c):
        return pl.ds(pl.multiple_of(c * span, span), span)

    def grads_load(c):
        return pltpu.make_async_copy(
            grads.at[span_of(c), :], grads_v.at[span_of(c), :], load_sem.at[c]
        )

    probe_load = pltpu.make_async_copy(probe, probe_v, load_sem.at[n_mp])
    acts_load = pltpu.make_async_copy(acts, acts_v, load_sem.at[n_mp + 1])
    probe_load.start()
    for i in range(n_mp):
        grads_load(lax.rem(me_m + 1 + i, n_mp)).start()
    acts_load.start()

    barrier = pltpu.get_barrier_semaphore()
    for i in range(1, n_mp):
        pl.semaphore_signal(
            barrier, inc=1, device_id={"mp": lax.rem(me_m + i, n_mp)}, device_id_type=MESH
        )
    for i in range(1, n_dp):
        pl.semaphore_signal(
            barrier, inc=1, device_id={"dp": lax.rem(me_d + i, n_dp)}, device_id_type=MESH
        )
    probe_load.wait()
    pl.semaphore_wait(barrier, n_mp + n_dp - 2)

    def copy(axis, src, dst, send, recv, peer):
        return pltpu.make_async_remote_copy(
            src_ref=src, dst_ref=dst, send_sem=send, recv_sem=recv,
            device_id={axis: peer}, device_id_type=MESH,
        )

    def gather_rows(s, piece):
        target = rows[s].at[:, span_of(me_m)]
        target[...] = piece.astype(BF16)

        def send(i, _):
            peer = lax.rem(me_m + i, n_mp)
            copy("mp", target, target, mp_send.at[s, 1, peer], mp_recv.at[s, 1, me_m], peer).start()
            return 0

        def wait(i, _):
            peer = lax.rem(me_m + i, n_mp)
            theirs = rows[s].at[:, span_of(peer)]
            copy("mp", target, theirs, mp_send.at[s, 1, peer], mp_recv.at[s, 1, peer], peer).wait()
            return 0

        lax.fori_loop(1, n_mp, send, 0)
        lax.fori_loop(1, n_mp, wait, 0)

    def scatter_rows(s, product, first, last):
        def body(i, _):
            c = lax.rem(me_m + i, n_mp)
            parts[s].at[c][...] = product(c).astype(BF16)

            @pl.when(i < n_mp)
            def _():
                copy(
                    "mp", parts[s].at[c], cames[s].at[me_m],
                    mp_send.at[s, 0, c], mp_recv.at[s, 0, me_m], c,
                ).start()

            return 0

        lax.fori_loop(first, last, body, 0)

    def collect_rows(s):
        def add(i, total):
            peer = lax.rem(me_m + i, n_mp)
            copy(
                "mp", parts[s].at[peer], cames[s].at[peer],
                mp_send.at[s, 0, peer], mp_recv.at[s, 0, peer], peer,
            ).wait()
            return total + cames[s].at[peer][...].astype(F32)

        return lax.fori_loop(1, n_mp, add, parts[s].at[me_m][...].astype(F32))

    def sum_tokens(s, field):
        width = field.shape[1] // n_dp

        def cols(j):
            return pl.ds(pl.multiple_of(j * width, 128), width)

        def body(i, _):
            j = lax.rem(me_d + i, n_dp)
            sents[s].at[j][...] = jnp.dot(
                rows[s][...], field[:, cols(j)], preferred_element_type=F32
            ).astype(BF16)

            @pl.when(i < n_dp)
            def _():
                copy(
                    "dp", sents[s].at[j], gots[s].at[me_d],
                    dp_send.at[s, 0, j], dp_recv.at[s, 0, me_d], j,
                ).start()

            return 0

        lax.fori_loop(1, n_dp + 1, body, 0)
        total = sents[s].at[me_d][...].astype(F32)
        for i in range(1, n_dp):
            peer = lax.rem(me_d + i, n_dp)
            copy(
                "dp", sents[s].at[peer], gots[s].at[peer],
                dp_send.at[s, 0, peer], dp_recv.at[s, 0, peer], peer,
            ).wait()
            total = total + gots[s].at[peer][...].astype(F32)
        target = sketches[s].at[:, cols(me_d)]
        target[...] = total.astype(BF16)
        for i in range(1, n_dp):
            peer = lax.rem(me_d + i, n_dp)
            copy("dp", target, target, dp_send.at[s, 1, peer], dp_recv.at[s, 1, me_d], peer).start()
        for i in range(1, n_dp):
            peer = lax.rem(me_d + i, n_dp)
            theirs = sketches[s].at[:, cols(peer)]
            copy("dp", target, theirs, dp_send.at[s, 1, peer], dp_recv.at[s, 1, peer], peer).wait()

    g_rows = k // n_mp

    def g_span(c):
        return pl.ds(pl.multiple_of(c * g_rows, g_rows), g_rows)

    def gram_start(s):
        sketch = sketches[s][...]
        gram_part.at[s][...] = lax.dot_general(
            sketch, sketch, (((1,), (1,)), ((), ())), preferred_element_type=F32
        )
        gram_came.at[s, me_m][...] = gram_part.at[s, g_span(me_m), :][...]
        for i in range(1, n_mp):
            peer = lax.rem(me_m + i, n_mp)
            copy(
                "mp", gram_part.at[s, g_span(peer), :], gram_came.at[s, me_m],
                g_send.at[s, 0, peer], g_recv.at[s, 0, me_m], peer,
            ).start()

    def gram_middle(s):
        for i in range(1, n_mp):
            peer = lax.rem(me_m + i, n_mp)
            copy(
                "mp", gram_part.at[s, g_span(peer), :], gram_came.at[s, peer],
                g_send.at[s, 0, peer], g_recv.at[s, 0, peer], peer,
            ).wait()
        target = gram_all.at[s, g_span(me_m), :]
        total = gram_came.at[s, 0][...]
        for i in range(1, n_mp):
            total = total + gram_came.at[s, i][...]
        target[...] = total
        for i in range(1, n_mp):
            peer = lax.rem(me_m + i, n_mp)
            copy("mp", target, target, g_send.at[s, 1, peer], g_recv.at[s, 1, me_m], peer).start()

    def gram_end(s):
        target = gram_all.at[s, g_span(me_m), :]
        for i in range(1, n_mp):
            peer = lax.rem(me_m + i, n_mp)
            theirs = gram_all.at[s, g_span(peer), :]
            copy("mp", target, theirs, g_send.at[s, 1, peer], g_recv.at[s, 1, peer], peer).wait()
        factor[...] = inverse_factor(gram_all.at[s][...])

    def probe_product(c):
        grads_load(c).wait()
        return jnp.dot(grads_v[span_of(c), :], probe_v[...], preferred_element_type=F32)

    scatter_rows(0, probe_product, 1, n_mp + 1)
    gather_rows(0, collect_rows(0).T)
    acts_load.wait()

    for s, (field, into) in enumerate(((acts_v, acts_v), (grads_v, grads_v), (acts_v, acts_v))):
        sum_tokens(s, field)
        gram_start(s)

        def product(c, s=s, into=into):
            return lax.dot_general(
                into[span_of(c), :], sketches[s][...],
                (((1,), (1,)), ((), ())), preferred_element_type=F32,
            )

        scatter_rows(s + 1, product, 1, n_mp // 2 + 1)
        gram_middle(s)
        scatter_rows(s + 1, product, n_mp // 2 + 1, n_mp + 1)
        gram_end(s)
        total = collect_rows(s + 1)
        gather_rows(
            s + 1,
            lax.dot_general(
                factor[...], total, (((1,), (1,)), ((), ())),
                precision=lax.Precision.HIGHEST, preferred_element_type=F32,
            ),
        )
    basis_t[...] = jnp.dot(
        factor[...], sk2[...].astype(F32),
        precision=lax.Precision.HIGHEST, preferred_element_type=F32,
    )
    sum_tokens(3, grads_v)


def fused(n_dp, n_mp, activations, output_grads, probe_matrix):
    tokens, features = activations.shape
    units, k = probe_matrix.shape
    span = tokens // n_mp
    widths = (features, units, features, units)
    any_space = pl.BlockSpec(memory_space=pl.ANY)
    vmem = pl.BlockSpec(memory_space=pltpu.VMEM)
    pieces = [pltpu.VMEM((n_mp, span, k), BF16)] * 4
    columns = [pltpu.VMEM((n_dp, k, w // n_dp), BF16) for w in widths]
    basis_t, proj = pl.pallas_call(
        functools.partial(kernel, n_dp, n_mp),
        out_shape=(
            jax.ShapeDtypeStruct((k, features), F32),
            jax.ShapeDtypeStruct((k, units), BF16),
        ),
        in_specs=[any_space] * 3,
        out_specs=(vmem, vmem),
        scratch_shapes=[
            pltpu.VMEM(activations.shape, BF16),
            pltpu.VMEM(output_grads.shape, BF16),
            pltpu.VMEM(probe_matrix.shape, BF16),
            *pieces,
            *pieces,
            *[pltpu.VMEM((k, tokens), BF16)] * 4,
            *columns,
            *columns,
            *[pltpu.VMEM((k, w), BF16) for w in widths[:3]],
            pltpu.VMEM((3, k, k), F32),
            pltpu.VMEM((3, n_mp, k // n_mp, k), F32),
            pltpu.VMEM((3, k, k), F32),
            pltpu.VMEM((k, k), F32),
            pltpu.SemaphoreType.DMA((n_mp + 2,)),
            pltpu.SemaphoreType.DMA((4, 2, n_mp)),
            pltpu.SemaphoreType.DMA((4, 2, n_mp)),
            pltpu.SemaphoreType.DMA((4, 2, n_dp)),
            pltpu.SemaphoreType.DMA((4, 2, n_dp)),
            pltpu.SemaphoreType.DMA((3, 2, n_mp)),
            pltpu.SemaphoreType.DMA((3, 2, n_mp)),
        ],
        compiler_params=pltpu.CompilerParams(
            collective_id=0, has_side_effects=True, vmem_limit_bytes=56 * 2**20
        ),
    )(activations, output_grads, probe_matrix)
    return (basis_t * jnp.sqrt(F32(H))).T, proj.astype(F32)


def contract_rows(left, right):
    return lax.dot_general(left, right, (((0,), (0,)), ((), ())), preferred_element_type=F32)


def token_total(partial_value):
    return lax.psum(partial_value.astype(BF16), "mp")


def orthonormalize(partial_value):
    summed = lax.psum(partial_value, "dp")
    gram = lax.dot_general(
        summed, summed, (((0,), (0,)), ((), ())),
        precision=lax.Precision.HIGHEST, preferred_element_type=F32,
    )
    factor = jnp.linalg.cholesky(lax.psum(gram, "mp"))
    return lax.linalg.triangular_solve(
        factor, summed, left_side=False, lower=True, transpose_a=True
    )


def separate(activations, output_grads, probe_matrix):
    def rows_of(field, columns):
        return token_total(jnp.dot(field, columns.astype(BF16), preferred_element_type=F32))

    first = orthonormalize(contract_rows(activations, rows_of(output_grads, probe_matrix)))
    second = orthonormalize(contract_rows(output_grads, rows_of(activations, first)))
    third = orthonormalize(contract_rows(activations, rows_of(output_grads, second)))
    projection = lax.psum(contract_rows(rows_of(activations, third), output_grads), "dp")
    return third * jnp.sqrt(F32(H)), projection


def solution(mesh):
    n_dp, n_mp = mesh.shape["dp"], mesh.shape["mp"]

    def on_device(activations, output_grads, probe_matrix):
        tokens, features = activations.shape
        units, k = probe_matrix.shape
        even = (
            features % (128 * n_dp) == 0
            and units % (128 * n_dp) == 0
            and tokens % (128 * n_mp) == 0
            and k % (8 * n_mp) == 0
        )
        run = functools.partial(fused, n_dp, n_mp) if even else separate
        return run(activations, output_grads, probe_matrix)

    in_specs = (P("dp", "mp"), P("dp", "mp"), P("mp", None))
    out_specs = (P("mp", None), P(None, "mp"))
    return jax.shard_map(
        on_device, mesh=mesh, in_specs=in_specs, out_specs=out_specs, check_vma=False
    )
```

```python
import functools

import jax
import jax.numpy as jnp
from jax import lax
from jax.experimental import pallas as pl
from jax.experimental.pallas import tpu as pltpu
from jax.sharding import PartitionSpec as P

H = 8192
F32, BF16 = jnp.float32, jnp.bfloat16
MESH = pl.DeviceIdType.MESH


def inverse_factor(gram):
    k = gram.shape[0]
    row_id = lax.broadcasted_iota(jnp.int32, (k, k), 0)
    lane_id = lax.broadcasted_iota(jnp.int32, (k, k), 1)
    lane_of = lax.broadcasted_iota(jnp.int32, (8, k), 1)
    row_of = lax.broadcasted_iota(jnp.int32, (k, 1), 0)
    group_id = lax.broadcasted_iota(jnp.int32, (k // 8, 8, k), 0)
    eye = row_id == lane_id

    def group_of(x, g):
        return jnp.sum(jnp.where(group_id == g, x.reshape(k // 8, 8, k), 0.0), axis=0)

    def lane_at(x, lanes, j):
        return jnp.sum(jnp.where(lanes == j, x, 0.0), axis=1, keepdims=True)

    def step(g, carry):
        m, e = carry
        for half in (0, 4):
            m_rows, e_rows = group_of(m, g), group_of(e, g)
            at = [8 * g + half + p for p in range(4)]
            cols = [lane_at(m, lane_id, j) for j in at]
            small = [lane_at(m_rows, lane_of, j) for j in at]
            rows = [m_rows[half + p : half + p + 1, :] for p in range(4)]
            done = [e_rows[half + p : half + p + 1, :] for p in range(4)]
            for p in range(4):
                inverse = 1.0 / small[p][half + p : half + p + 1, :]
                for q in range(p + 1, 4):
                    ratio = small[p][half + q : half + q + 1, :] * inverse
                    rows[q] = rows[q] - ratio * rows[p]
                    done[q] = done[q] - ratio * done[p]
                    cols[q] = cols[q] - ratio * cols[p]
                    small[q] = small[q] - ratio * small[p]
                scale = jnp.where(row_of > at[p], cols[p] * inverse, 0.0)
                m = m - scale * rows[p]
                e = e - scale * done[p]
        return m, e

    m, e = lax.fori_loop(0, k // 8, step, (gram, jnp.where(eye, 1.0, 0.0).astype(F32)))
    pivots = jnp.sum(jnp.where(eye, m, 0.0), axis=1, keepdims=True)
    return e * lax.rsqrt(pivots)


def kernel(
    n_dp, n_mp, acts, grads, probe, basis_t, proj,
    acts_v, grads_v, probe_v,
    part0, part1, part2, part3, came0, came1, came2, came3, rows0, rows1, rows2, rows3,
    sent0, sent2, got0, got2, sk0, sk1, sk2,
    up_part, up_came, cross_came, held,
    gram_part, gram_came, gram_all, factor,
    load_sem, mp_send, mp_recv, dp_send, dp_recv, g_send, g_recv,
    out_send, in_send, up_recv, cross_recv, done_recv,
):
    me_d, me_m = lax.axis_index("dp"), lax.axis_index("mp")
    tokens, k = acts_v.shape[0], probe_v.shape[1]
    span = tokens // n_mp
    parts, cames = (part0, part1, part2, part3), (came0, came1, came2, came3)
    rows = (rows0, rows1, rows2, rows3)
    sents, gots = (sent0, None, sent2, None), (got0, None, got2, None)
    sketches = (sk0, sk1, sk2, proj)

    def span_of(c):
        return pl.ds(pl.multiple_of(c * span, span), span)

    def grads_load(c):
        return pltpu.make_async_copy(
            grads.at[span_of(c), :], grads_v.at[span_of(c), :], load_sem.at[c]
        )

    probe_load = pltpu.make_async_copy(probe, probe_v, load_sem.at[n_mp])
    acts_load = pltpu.make_async_copy(acts, acts_v, load_sem.at[n_mp + 1])
    probe_load.start()
    for i in range(n_mp):
        grads_load(lax.rem(me_m + 1 + i, n_mp)).start()
    acts_load.start()

    barrier = pltpu.get_barrier_semaphore()
    for i in range(1, n_mp):
        pl.semaphore_signal(
            barrier, inc=1, device_id={"mp": lax.rem(me_m + i, n_mp)}, device_id_type=MESH
        )
    for i in range(1, n_dp):
        pl.semaphore_signal(
            barrier, inc=1, device_id={"dp": lax.rem(me_d + i, n_dp)}, device_id_type=MESH
        )
    probe_load.wait()
    pl.semaphore_wait(barrier, n_mp + n_dp - 2)

    def copy(axis, src, dst, send, recv, peer):
        return pltpu.make_async_remote_copy(
            src_ref=src, dst_ref=dst, send_sem=send, recv_sem=recv,
            device_id={axis: peer}, device_id_type=MESH,
        )

    def gather_rows(s, piece, meanwhile=None):
        target = rows[s].at[:, span_of(me_m)]
        target[...] = piece.astype(BF16)

        def send(i, _):
            peer = lax.rem(me_m + i, n_mp)
            copy("mp", target, target, mp_send.at[s, 1, peer], mp_recv.at[s, 1, me_m], peer).start()
            return 0

        def wait(i, _):
            peer = lax.rem(me_m + i, n_mp)
            theirs = rows[s].at[:, span_of(peer)]
            copy("mp", target, theirs, mp_send.at[s, 1, peer], mp_recv.at[s, 1, peer], peer).wait()
            return 0

        lax.fori_loop(1, n_mp, send, 0)
        if meanwhile is not None:
            meanwhile()
        lax.fori_loop(1, n_mp, wait, 0)

    def scatter_rows(s, product, first, last):
        def body(i, _):
            c = lax.rem(me_m + i, n_mp)
            parts[s].at[c][...] = product(c).astype(BF16)

            @pl.when(i < n_mp)
            def _():
                copy(
                    "mp", parts[s].at[c], cames[s].at[me_m],
                    mp_send.at[s, 0, c], mp_recv.at[s, 0, me_m], c,
                ).start()

            return 0

        lax.fori_loop(first, last, body, 0)

    def collect_rows(s):
        def add(i, total):
            peer = lax.rem(me_m + i, n_mp)
            copy(
                "mp", parts[s].at[peer], cames[s].at[peer],
                mp_send.at[s, 0, peer], mp_recv.at[s, 0, peer], peer,
            ).wait()
            return total + cames[s].at[peer][...].astype(F32)

        return lax.fori_loop(1, n_mp, add, parts[s].at[me_m][...].astype(F32))

    def sum_tokens(s, field):
        width = field.shape[1] // n_dp

        def cols(j):
            return pl.ds(pl.multiple_of(j * width, 128), width)

        def body(i, _):
            j = lax.rem(me_d + i, n_dp)
            sents[s].at[j][...] = jnp.dot(
                rows[s][...], field[:, cols(j)], preferred_element_type=F32
            ).astype(BF16)

            @pl.when(i < n_dp)
            def _():
                copy(
                    "dp", sents[s].at[j], gots[s].at[me_d],
                    dp_send.at[s, 0, j], dp_recv.at[s, 0, me_d], j,
                ).start()

            return 0

        lax.fori_loop(1, n_dp + 1, body, 0)
        total = sents[s].at[me_d][...].astype(F32)
        for i in range(1, n_dp):
            peer = lax.rem(me_d + i, n_dp)
            copy(
                "dp", sents[s].at[peer], gots[s].at[peer],
                dp_send.at[s, 0, peer], dp_recv.at[s, 0, peer], peer,
            ).wait()
            total = total + gots[s].at[peer][...].astype(F32)
        target = sketches[s].at[:, cols(me_d)]
        target[...] = total.astype(BF16)
        for i in range(1, n_dp):
            peer = lax.rem(me_d + i, n_dp)
            copy("dp", target, target, dp_send.at[s, 1, peer], dp_recv.at[s, 1, me_d], peer).start()
        for i in range(1, n_dp):
            peer = lax.rem(me_d + i, n_dp)
            theirs = sketches[s].at[:, cols(peer)]
            copy("dp", target, theirs, dp_send.at[s, 1, peer], dp_recv.at[s, 1, peer], peer).wait()

    def sum_tokens_line(w, s, field):
        chunks, width = held.shape[1], held.shape[3]
        edge = (me_d == 0) | (me_d == n_dp - 1)
        inner = 1 + me_d // 3
        other, outer = 3 - me_d, 3 * (me_d - 1)

        def cols(half, t):
            return pl.ds(pl.multiple_of((half * chunks + t) * width, width), width)

        def product(half, t):
            return jnp.dot(rows[s][...], field[:, cols(half, t)], preferred_element_type=F32)

        def up(half, t, peer):
            return copy(
                "dp", up_part.at[w, half, t], up_came.at[w, half, t],
                out_send.at[w, half, t], up_recv.at[w, half, t], peer,
            )

        def cross(half, t):
            return copy(
                "dp", up_part.at[w, half, t], cross_came.at[w, t],
                in_send.at[w, 0, t], cross_recv.at[w, t], other,
            )

        def done(half, t, send, peer):
            chunk = sketches[s].at[:, cols(half, t)]
            return copy("dp", chunk, chunk, send, done_recv.at[w, half, t], peer)

        @pl.when(edge)
        def _():
            def give(t, _):
                for half in (2 - inner, inner - 1):
                    up_part.at[w, half, t][...] = product(half, t).astype(BF16)
                    up(half, t, inner).start()
                return 0

            def take(t, _):
                for half in (2 - inner, inner - 1):
                    up(half, t, inner).wait_send()
                    done(half, t, out_send.at[w, half, t], inner).wait_recv()
                return 0

            lax.fori_loop(0, chunks, give, 0)
            lax.fori_loop(0, chunks, take, 0)

        @pl.when(jnp.logical_not(edge))
        def _():
            mine, theirs = me_d - 1, 2 - me_d

            def body(t, _):
                @pl.when(t < chunks)
                def _():
                    total = product(theirs, t)
                    up(theirs, t, outer).wait_recv()
                    total = total + up_came.at[w, theirs, t][...].astype(F32)
                    up_part.at[w, theirs, t][...] = total.astype(BF16)
                    cross(theirs, t).start()
                    total = product(mine, t)
                    up(mine, t, outer).wait_recv()
                    held.at[w, t][...] = total + up_came.at[w, mine, t][...].astype(F32)

                @pl.when((t >= 1) & (t < chunks + 1))
                def _():
                    u = t - 1
                    cross(mine, u).wait_recv()
                    total = held.at[w, u][...] + cross_came.at[w, u][...].astype(F32)
                    sketches[s].at[:, cols(mine, u)][...] = total.astype(BF16)
                    done(mine, u, out_send.at[w, 1, u], other).start()
                    done(mine, u, out_send.at[w, 0, u], outer).start()

                @pl.when(t >= 2)
                def _():
                    u = t - 2
                    done(theirs, u, in_send.at[w, 1, u], other).wait_recv()
                    done(theirs, u, in_send.at[w, 1, u], outer).start()

                return 0

            def end(t, _):
                cross(theirs, t).wait_send()
                done(mine, t, out_send.at[w, 1, t], other).wait_send()
                done(mine, t, out_send.at[w, 0, t], outer).wait_send()
                done(theirs, t, in_send.at[w, 1, t], outer).wait_send()
                return 0

            lax.fori_loop(0, chunks + 2, body, 0)
            lax.fori_loop(0, chunks, end, 0)

    g_rows = k // n_mp

    def g_span(c):
        return pl.ds(pl.multiple_of(c * g_rows, g_rows), g_rows)

    def gram_start(s):
        sketch = sketches[s][...]
        gram_part.at[s][...] = lax.dot_general(
            sketch, sketch, (((1,), (1,)), ((), ())), preferred_element_type=F32
        )
        gram_came.at[s, me_m][...] = gram_part.at[s, g_span(me_m), :][...]
        for i in range(1, n_mp):
            peer = lax.rem(me_m + i, n_mp)
            copy(
                "mp", gram_part.at[s, g_span(peer), :], gram_came.at[s, me_m],
                g_send.at[s, 0, peer], g_recv.at[s, 0, me_m], peer,
            ).start()

    def gram_middle(s):
        for i in range(1, n_mp):
            peer = lax.rem(me_m + i, n_mp)
            copy(
                "mp", gram_part.at[s, g_span(peer), :], gram_came.at[s, peer],
                g_send.at[s, 0, peer], g_recv.at[s, 0, peer], peer,
            ).wait()
        target = gram_all.at[s, g_span(me_m), :]
        total = gram_came.at[s, 0][...]
        for i in range(1, n_mp):
            total = total + gram_came.at[s, i][...]
        target[...] = total
        for i in range(1, n_mp):
            peer = lax.rem(me_m + i, n_mp)
            copy("mp", target, target, g_send.at[s, 1, peer], g_recv.at[s, 1, me_m], peer).start()

    def gram_end(s):
        target = gram_all.at[s, g_span(me_m), :]
        for i in range(1, n_mp):
            peer = lax.rem(me_m + i, n_mp)
            theirs = gram_all.at[s, g_span(peer), :]
            copy("mp", target, theirs, g_send.at[s, 1, peer], g_recv.at[s, 1, peer], peer).wait()
        factor[...] = inverse_factor(gram_all.at[s][...])

    def probe_product(c):
        grads_load(c).wait()
        return jnp.dot(grads_v[span_of(c), :], probe_v[...], preferred_element_type=F32)

    scatter_rows(0, probe_product, 1, n_mp + 1)
    gather_rows(0, collect_rows(0).T)
    acts_load.wait()

    def write_basis():
        basis_t[...] = jnp.dot(
            factor[...], sk2[...].astype(F32),
            precision=lax.Precision.HIGHEST, preferred_element_type=F32,
        )

    for s, (field, into) in enumerate(((acts_v, acts_v), (grads_v, grads_v), (acts_v, acts_v))):
        if s == 1:
            sum_tokens_line(0, s, field)
        else:
            sum_tokens(s, field)
        gram_start(s)

        def product(c, s=s, into=into):
            return lax.dot_general(
                into[span_of(c), :], sketches[s][...],
                (((1,), (1,)), ((), ())), preferred_element_type=F32,
            )

        scatter_rows(s + 1, product, 1, n_mp // 2 + 1)
        gram_middle(s)
        scatter_rows(s + 1, product, n_mp // 2 + 1, n_mp + 1)
        gram_end(s)
        total = collect_rows(s + 1)
        gather_rows(
            s + 1,
            lax.dot_general(
                factor[...], total, (((1,), (1,)), ((), ())),
                precision=lax.Precision.HIGHEST, preferred_element_type=F32,
            ),
            write_basis if s == 2 else None,
        )
    sum_tokens_line(1, 3, grads_v)


def fused(n_dp, n_mp, activations, output_grads, probe_matrix):
    tokens, features = activations.shape
    units, k = probe_matrix.shape
    span = tokens // n_mp
    chunk, chunks = 256, units // 512
    any_space = pl.BlockSpec(memory_space=pl.ANY)
    vmem = pl.BlockSpec(memory_space=pltpu.VMEM)
    pieces = [pltpu.VMEM((n_mp, span, k), BF16)] * 4
    columns = [pltpu.VMEM((n_dp, k, features // n_dp), BF16)] * 2
    basis_t, proj = pl.pallas_call(
        functools.partial(kernel, n_dp, n_mp),
        out_shape=(
            jax.ShapeDtypeStruct((k, features), F32),
            jax.ShapeDtypeStruct((k, units), BF16),
        ),
        in_specs=[any_space] * 3,
        out_specs=(vmem, vmem),
        scratch_shapes=[
            pltpu.VMEM(activations.shape, BF16),
            pltpu.VMEM(output_grads.shape, BF16),
            pltpu.VMEM(probe_matrix.shape, BF16),
            *pieces,
            *pieces,
            *[pltpu.VMEM((k, tokens), BF16)] * 4,
            *columns,
            *columns,
            *[pltpu.VMEM((k, w), BF16) for w in (features, units, features)],
            pltpu.VMEM((2, 2, chunks, k, chunk), BF16),
            pltpu.VMEM((2, 2, chunks, k, chunk), BF16),
            pltpu.VMEM((2, chunks, k, chunk), BF16),
            pltpu.VMEM((2, chunks, k, chunk), F32),
            pltpu.VMEM((3, k, k), F32),
            pltpu.VMEM((3, n_mp, k // n_mp, k), F32),
            pltpu.VMEM((3, k, k), F32),
            pltpu.VMEM((k, k), F32),
            pltpu.SemaphoreType.DMA((n_mp + 2,)),
            pltpu.SemaphoreType.DMA((4, 2, n_mp)),
            pltpu.SemaphoreType.DMA((4, 2, n_mp)),
            pltpu.SemaphoreType.DMA((4, 2, n_dp)),
            pltpu.SemaphoreType.DMA((4, 2, n_dp)),
            pltpu.SemaphoreType.DMA((3, 2, n_mp)),
            pltpu.SemaphoreType.DMA((3, 2, n_mp)),
            pltpu.SemaphoreType.DMA((2, 2, chunks)),
            pltpu.SemaphoreType.DMA((2, 2, chunks)),
            pltpu.SemaphoreType.DMA((2, 2, chunks)),
            pltpu.SemaphoreType.DMA((2, chunks)),
            pltpu.SemaphoreType.DMA((2, 2, chunks)),
        ],
        compiler_params=pltpu.CompilerParams(
            collective_id=0, has_side_effects=True, vmem_limit_bytes=56 * 2**20
        ),
    )(activations, output_grads, probe_matrix)
    return (basis_t * jnp.sqrt(F32(H))).T, proj.astype(F32)


def contract_rows(left, right):
    return lax.dot_general(left, right, (((0,), (0,)), ((), ())), preferred_element_type=F32)


def token_total(partial_value):
    return lax.psum(partial_value.astype(BF16), "mp")


def orthonormalize(partial_value):
    summed = lax.psum(partial_value, "dp")
    gram = lax.dot_general(
        summed, summed, (((0,), (0,)), ((), ())),
        precision=lax.Precision.HIGHEST, preferred_element_type=F32,
    )
    factor = jnp.linalg.cholesky(lax.psum(gram, "mp"))
    return lax.linalg.triangular_solve(
        factor, summed, left_side=False, lower=True, transpose_a=True
    )


def separate(activations, output_grads, probe_matrix):
    def rows_of(field, columns):
        return token_total(jnp.dot(field, columns.astype(BF16), preferred_element_type=F32))

    first = orthonormalize(contract_rows(activations, rows_of(output_grads, probe_matrix)))
    second = orthonormalize(contract_rows(output_grads, rows_of(activations, first)))
    third = orthonormalize(contract_rows(activations, rows_of(output_grads, second)))
    projection = lax.psum(contract_rows(rows_of(activations, third), output_grads), "dp")
    return third * jnp.sqrt(F32(H)), projection


def solution(mesh):
    n_dp, n_mp = mesh.shape["dp"], mesh.shape["mp"]

    def on_device(activations, output_grads, probe_matrix):
        tokens, features = activations.shape
        units, k = probe_matrix.shape
        even = (
            n_dp == 4
            and features % (128 * n_dp) == 0
            and units % 512 == 0
            and tokens % (128 * n_mp) == 0
            and k % (8 * n_mp) == 0
        )
        run = functools.partial(fused, n_dp, n_mp) if even else separate
        return run(activations, output_grads, probe_matrix)

    in_specs = (P("dp", "mp"), P("dp", "mp"), P("mp", None))
    out_specs = (P("mp", None), P(None, "mp"))
    return jax.shard_map(
        on_device, mesh=mesh, in_specs=in_specs, out_specs=out_specs, check_vma=False
    )
```

```python
import functools

import jax
import jax.numpy as jnp
from jax import lax
from jax.experimental import pallas as pl
from jax.experimental.pallas import tpu as pltpu
from jax.sharding import PartitionSpec as P

H = 8192
F32, BF16 = jnp.float32, jnp.bfloat16
MESH = pl.DeviceIdType.MESH


def inverse_factor(gram):
    k = gram.shape[0]
    lane_of = lax.broadcasted_iota(jnp.int32, (8, k), 1)
    m, e = gram, jnp.where(
        lax.broadcasted_iota(jnp.int32, (k, k), 0) == lax.broadcasted_iota(jnp.int32, (k, k), 1), 1.0, 0.0
    ).astype(F32)
    finished = []
    segment = k // 4

    def lane_at(x, lanes, j):
        return jnp.sum(jnp.where(lanes == j, x, 0.0), axis=1, keepdims=True)

    for first in range(0, k, segment):
        height = k - first
        lane_id = lax.broadcasted_iota(jnp.int32, (height, k), 1)
        row_id = first + lax.broadcasted_iota(jnp.int32, (height, k), 0)
        row_of = first + lax.broadcasted_iota(jnp.int32, (height, 1), 0)
        group_id = first // 8 + lax.broadcasted_iota(jnp.int32, (height // 8, 8, k), 0)

        def group_of(x, g, height=height, group_id=group_id):
            x = x.reshape(height // 8, 8, k)
            return jnp.sum(jnp.where(group_id == g, x, 0.0), axis=0)

        def step(g, carry, lane_id=lane_id, row_of=row_of, group_of=group_of):
            m, e = carry
            for half in (0, 4):
                m_rows, e_rows = group_of(m, g), group_of(e, g)
                at = [8 * g + half + p for p in range(4)]
                cols = [lane_at(m, lane_id, j) for j in at]
                small = [lane_at(m_rows, lane_of, j) for j in at]
                rows = [m_rows[half + p : half + p + 1, :] for p in range(4)]
                done = [e_rows[half + p : half + p + 1, :] for p in range(4)]
                for p in range(4):
                    inverse = 1.0 / small[p][half + p : half + p + 1, :]
                    for q in range(p + 1, 4):
                        ratio = small[p][half + q : half + q + 1, :] * inverse
                        rows[q] = rows[q] - ratio * rows[p]
                        done[q] = done[q] - ratio * done[p]
                        cols[q] = cols[q] - ratio * cols[p]
                        small[q] = small[q] - ratio * small[p]
                    scale = jnp.where(row_of > at[p], cols[p] * inverse, 0.0)
                    m = m - scale * rows[p]
                    e = e - scale * done[p]
            return m, e

        m, e = lax.fori_loop(first // 8, (first + segment) // 8, step, (m, e))
        top = jnp.where(lane_id == row_id, m, 0.0)[:segment]
        finished.append(e[:segment] * lax.rsqrt(jnp.sum(top, axis=1, keepdims=True)))
        m, e = m[segment:], e[segment:]
    return jnp.concatenate(finished, axis=0)


def kernel(
    n_dp, n_mp, acts, grads, probe, basis, proj,
    acts_v, grads_v, probe_v,
    part0, part1, part2, part3, came0, came1, came2, came3, rows0, rows1, rows2, rows3,
    sent0, sent2, got0, got2, sk0, sk1, sk2,
    up_part, up_came, cross_came, row_sums,
    gram_part, gram_came, gram_sums, gram_all, factor,
    load_sem, mp_send, mp_recv, dp_send, dp_recv, g_send, g_recv, gd_send, gd_recv,
    out_send, in_send, up_recv, cross_recv, done_recv,
):
    me_d, me_m = lax.axis_index("dp"), lax.axis_index("mp")
    tokens, k = acts_v.shape[0], probe_v.shape[1]
    span = tokens // n_mp
    parts, cames = (part0, part1, part2, part3), (came0, came1, came2, came3)
    rows = (rows0, rows1, rows2, rows3)
    sents, gots = (sent0, None, sent2, None), (got0, None, got2, None)
    sketches = (sk0, sk1, sk2, proj)

    def span_of(c):
        return pl.ds(pl.multiple_of(c * span, span), span)

    def grads_load(c):
        return pltpu.make_async_copy(
            grads.at[span_of(c), :], grads_v.at[span_of(c), :], load_sem.at[c]
        )

    probe_load = pltpu.make_async_copy(probe, probe_v, load_sem.at[n_mp])
    acts_load = pltpu.make_async_copy(acts, acts_v, load_sem.at[n_mp + 1])
    probe_load.start()
    for i in range(n_mp):
        grads_load(lax.rem(me_m + 1 + i, n_mp)).start()
    acts_load.start()

    barrier = pltpu.get_barrier_semaphore()
    for i in range(1, n_mp):
        pl.semaphore_signal(
            barrier, inc=1, device_id={"mp": lax.rem(me_m + i, n_mp)}, device_id_type=MESH
        )
    for i in range(1, n_dp):
        pl.semaphore_signal(
            barrier, inc=1, device_id={"dp": lax.rem(me_d + i, n_dp)}, device_id_type=MESH
        )
    probe_load.wait()
    pl.semaphore_wait(barrier, n_mp + n_dp - 2)

    def copy(axis, src, dst, send, recv, peer):
        return pltpu.make_async_remote_copy(
            src_ref=src, dst_ref=dst, send_sem=send, recv_sem=recv,
            device_id={axis: peer}, device_id_type=MESH,
        )

    def gather_rows(s, piece, meanwhile=None):
        target = rows[s].at[:, span_of(me_m)]
        target[...] = piece.astype(BF16)

        pair = me_m + 1 - 2 * lax.rem(me_m, 2)
        peers = [lax.rem(me_m + i, n_mp) for i in range(2, n_mp, 2)] + [pair]

        def far(chunk, send, owner, peer):
            return copy("mp", chunk, chunk, mp_send.at[s, 1, send], mp_recv.at[s, 1, owner], peer)

        def twin(peer):
            return peer + 1 - 2 * lax.rem(peer, 2)

        for peer in peers:
            far(target, peer, me_m, peer).start()
        for peer in peers[:-1]:
            theirs = rows[s].at[:, span_of(peer)]
            far(theirs, peer, peer, peer).wait_recv()
            far(theirs, twin(peer), peer, pair).start()
        if meanwhile is not None:
            meanwhile()
        for peer in peers[:-1]:
            theirs = rows[s].at[:, span_of(twin(peer))]
            far(theirs, twin(peer), twin(peer), pair).wait()
            far(target, peer, me_m, peer).wait_send()
        far(rows[s].at[:, span_of(pair)], pair, pair, pair).wait()

    def scatter_rows(s, product, first, last):
        def body(i, _):
            c = lax.rem(me_m + i, n_mp)
            parts[s].at[c][...] = product(c).astype(BF16)

            @pl.when(i < n_mp)
            def _():
                copy(
                    "mp", parts[s].at[c], cames[s].at[me_m],
                    mp_send.at[s, 0, c], mp_recv.at[s, 0, me_m], c,
                ).start()

            return 0

        lax.fori_loop(first, last, body, 0)

    def collect_rows(s):
        def add(i, total):
            peer = lax.rem(me_m + i, n_mp)
            copy(
                "mp", parts[s].at[peer], cames[s].at[peer],
                mp_send.at[s, 0, peer], mp_recv.at[s, 0, peer], peer,
            ).wait()
            return total + cames[s].at[peer][...].astype(F32)

        return lax.fori_loop(1, n_mp, add, parts[s].at[me_m][...].astype(F32))

    def sum_tokens(s, field):
        width = field.shape[1] // n_dp

        def cols(j):
            return pl.ds(pl.multiple_of(j * width, 128), width)

        def body(i, _):
            j = lax.rem(me_d + i, n_dp)
            sents[s].at[j][...] = jnp.dot(
                rows[s][...], field[:, cols(j)], preferred_element_type=F32
            ).astype(BF16)

            @pl.when(i < n_dp)
            def _():
                copy(
                    "dp", sents[s].at[j], gots[s].at[me_d],
                    dp_send.at[s, 0, j], dp_recv.at[s, 0, me_d], j,
                ).start()

            return 0

        lax.fori_loop(1, n_dp + 1, body, 0)
        total = sents[s].at[me_d][...].astype(F32)
        for i in range(1, n_dp):
            peer = lax.rem(me_d + i, n_dp)
            copy(
                "dp", sents[s].at[peer], gots[s].at[peer],
                dp_send.at[s, 0, peer], dp_recv.at[s, 0, peer], peer,
            ).wait()
            total = total + gots[s].at[peer][...].astype(F32)
        share = total.astype(BF16)
        gram_part.at[s][...] = gram_of(share)
        gram_start(s)
        target = sketches[s].at[cols(me_d), :]
        target[...] = total.T.astype(BF16)
        for i in range(1, n_dp):
            peer = lax.rem(me_d + i, n_dp)
            copy("dp", target, target, dp_send.at[s, 1, peer], dp_recv.at[s, 1, me_d], peer).start()
        gram_across(s)
        gram_middle(s)
        for i in range(1, n_dp):
            peer = lax.rem(me_d + i, n_dp)
            theirs = sketches[s].at[cols(peer), :]
            copy("dp", target, theirs, dp_send.at[s, 1, peer], dp_recv.at[s, 1, peer], peer).wait()

    def sum_tokens_line(w, s, field):
        chunks, width = cross_came.shape[1], cross_came.shape[3]
        edge = (me_d == 0) | (me_d == n_dp - 1)
        inner = 1 + me_d // 3
        other, outer = 3 - me_d, 3 * (me_d - 1)

        def cols(half, t):
            return pl.ds(pl.multiple_of((half * chunks + t) * width, width), width)

        def product(half, t):
            return jnp.dot(rows[s][...], field[:, cols(half, t)], preferred_element_type=F32)

        def up(half, t, peer):
            return copy(
                "dp", up_part.at[w, half, t], up_came.at[w, half, t],
                out_send.at[w, half, t], up_recv.at[w, half, t], peer,
            )

        def cross(half, t):
            return copy(
                "dp", up_part.at[w, half, t], cross_came.at[w, t],
                in_send.at[w, 0, t], cross_recv.at[w, t], other,
            )

        def done(half, t, send, peer):
            if s == 3:
                chunk = sketches[s].at[:, cols(half, t)]
            else:
                chunk = sketches[s].at[cols(half, t), :]
            return copy("dp", chunk, chunk, send, done_recv.at[w, half, t], peer)

        if s != 3:
            gram_part.at[s][...] = jnp.zeros((k, k), F32)

        def add_rows(half, t):
            if s != 3:
                chunk = cols(half, t)
                row_sums[...] += jnp.dot(
                    field[:, chunk], sketches[s][chunk, :], preferred_element_type=F32
                )

        if s != 3:
            row_sums[...] = jnp.zeros_like(row_sums)

        @pl.when(edge)
        def _():
            near, far = inner - 1, 2 - inner

            def give(half, t):
                up_part.at[w, half, t][...] = product(half, t).astype(BF16)
                up(half, t, inner).start()

            def take(half, t):
                up(half, t, inner).wait_send()
                done(half, t, out_send.at[w, half, t], inner).wait_recv()
                add_rows(half, t)

            def body(t, _):
                @pl.when(t < chunks)
                def _():
                    give(far, t)

                @pl.when((t >= 1) & (t < chunks + 1))
                def _():
                    give(near, t - 1)

                @pl.when((t >= 3) & (t < chunks + 3))
                def _():
                    take(near, t - 3)

                @pl.when(t >= 4)
                def _():
                    take(far, t - 4)

                return 0

            lax.fori_loop(0, chunks + 4, body, 0)

        @pl.when(jnp.logical_not(edge))
        def _():
            mine, theirs = me_d - 1, 2 - me_d

            def body(t, _):
                @pl.when(t < chunks)
                def _():
                    total = product(theirs, t)
                    up(theirs, t, outer).wait_recv()
                    total = total + up_came.at[w, theirs, t][...].astype(F32)
                    up_part.at[w, theirs, t][...] = total.astype(BF16)
                    cross(theirs, t).start()

                @pl.when((t >= 1) & (t < chunks + 1))
                def _():
                    u = t - 1
                    total = product(mine, u)
                    up(mine, u, outer).wait_recv()
                    cross(mine, u).wait_recv()
                    total = total + up_came.at[w, mine, u][...].astype(F32)
                    total = total + cross_came.at[w, u][...].astype(F32)
                    if s == 3:
                        sketches[s].at[:, cols(mine, u)][...] = total.astype(BF16)
                    else:
                        sketches[s].at[cols(mine, u), :][...] = total.T.astype(BF16)
                    done(mine, u, out_send.at[w, 1, u], other).start()
                    done(mine, u, out_send.at[w, 0, u], outer).start()
                    if s != 3:
                        gram_part.at[s][...] += gram_of(total.astype(BF16))
                    add_rows(mine, u)

                @pl.when(t >= 2)
                def _():
                    u = t - 2
                    done(theirs, u, in_send.at[w, 1, u], other).wait_recv()
                    done(theirs, u, in_send.at[w, 1, u], outer).start()
                    add_rows(theirs, u)

                return 0

            def end(t, _):
                cross(theirs, t).wait_send()
                done(mine, t, out_send.at[w, 1, t], other).wait_send()
                done(mine, t, out_send.at[w, 0, t], outer).wait_send()
                done(theirs, t, in_send.at[w, 1, t], outer).wait_send()
                return 0

            lax.fori_loop(0, chunks + 2, body, 0)
            lax.fori_loop(0, chunks, end, 0)

    g_rows = k // n_mp

    def g_span(c):
        return pl.ds(pl.multiple_of(c * g_rows, g_rows), g_rows)

    def gram_of(share):
        return lax.dot_general(
            share, share, (((1,), (1,)), ((), ())), preferred_element_type=F32
        )

    def gram_start(s):
        gram_came.at[s, me_m][...] = gram_part.at[s, g_span(me_m), :][...]
        for i in range(1, n_mp):
            peer = lax.rem(me_m + i, n_mp)
            copy(
                "mp", gram_part.at[s, g_span(peer), :], gram_came.at[s, me_m],
                g_send.at[s, 0, peer], g_recv.at[s, 0, me_m], peer,
            ).start()

    def gram_across(s):
        for i in range(1, n_mp):
            peer = lax.rem(me_m + i, n_mp)
            copy(
                "mp", gram_part.at[s, g_span(peer), :], gram_came.at[s, peer],
                g_send.at[s, 0, peer], g_recv.at[s, 0, peer], peer,
            ).wait()
        total = gram_came.at[s, 0][...]
        for i in range(1, n_mp):
            total = total + gram_came.at[s, i][...]
        target = gram_sums.at[s, me_d]
        target[...] = total
        for i in range(1, n_dp):
            peer = lax.rem(me_d + i, n_dp)
            copy("dp", target, target, gd_send.at[s, peer], gd_recv.at[s, me_d], peer).start()

    def gram_middle(s):
        for i in range(1, n_dp):
            peer = lax.rem(me_d + i, n_dp)
            theirs = gram_sums.at[s, peer]
            copy("dp", gram_sums.at[s, me_d], theirs, gd_send.at[s, peer], gd_recv.at[s, peer], peer).wait()
        target = gram_all.at[s, g_span(me_m), :]
        total = gram_sums.at[s, 0][...]
        for i in range(1, n_dp):
            total = total + gram_sums.at[s, i][...]
        target[...] = total
        for i in range(1, n_mp):
            peer = lax.rem(me_m + i, n_mp)
            copy("mp", target, target, g_send.at[s, 1, peer], g_recv.at[s, 1, me_m], peer).start()

    def gram_end(s):
        target = gram_all.at[s, g_span(me_m), :]
        for i in range(1, n_mp):
            peer = lax.rem(me_m + i, n_mp)
            theirs = gram_all.at[s, g_span(peer), :]
            copy("mp", target, theirs, g_send.at[s, 1, peer], g_recv.at[s, 1, peer], peer).wait()
        factor[...] = inverse_factor(gram_all.at[s][...])

    def probe_product(c):
        grads_load(c).wait()
        return jnp.dot(grads_v[span_of(c), :], probe_v[...], preferred_element_type=F32)

    scatter_rows(0, probe_product, 1, n_mp + 1)
    gather_rows(0, collect_rows(0).T)
    acts_load.wait()

    def write_basis():
        basis[...] = lax.dot_general(
            sk2[...].astype(F32), factor[...], (((1,), (1,)), ((), ())),
            precision=lax.Precision.HIGHEST, preferred_element_type=F32,
        )

    for s, (field, into) in enumerate(((acts_v, acts_v), (grads_v, grads_v), (acts_v, acts_v))):
        if s == 1:
            sum_tokens_line(0, s, field)
            gram_start(s)
        else:
            sum_tokens(s, field)

        def product(c, s=s, into=into):
            if s == 1:
                return row_sums[span_of(c), :]
            return jnp.dot(
                into[span_of(c), :], sketches[s][...], preferred_element_type=F32
            )

        if s == 1:
            scatter_rows(s + 1, product, 1, n_mp + 1)
            gram_across(s)
            gram_middle(s)
        else:
            scatter_rows(s + 1, product, 1, n_mp + 1)
        gram_end(s)
        total = collect_rows(s + 1)
        gather_rows(
            s + 1,
            lax.dot_general(
                factor[...], total, (((1,), (1,)), ((), ())),
                precision=lax.Precision.HIGHEST, preferred_element_type=F32,
            ),
            write_basis if s == 2 else None,
        )
    sum_tokens_line(1, 3, grads_v)


def fused(n_dp, n_mp, activations, output_grads, probe_matrix):
    tokens, features = activations.shape
    units, k = probe_matrix.shape
    span = tokens // n_mp
    chunk, chunks = 256, units // 512
    any_space = pl.BlockSpec(memory_space=pl.ANY)
    vmem = pl.BlockSpec(memory_space=pltpu.VMEM)
    pieces = [pltpu.VMEM((n_mp, span, k), BF16)] * 4
    columns = [pltpu.VMEM((n_dp, k, features // n_dp), BF16)] * 2
    basis, proj = pl.pallas_call(
        functools.partial(kernel, n_dp, n_mp),
        out_shape=(
            jax.ShapeDtypeStruct((features, k), F32),
            jax.ShapeDtypeStruct((k, units), BF16),
        ),
        in_specs=[any_space] * 3,
        out_specs=(vmem, vmem),
        scratch_shapes=[
            pltpu.VMEM(activations.shape, BF16),
            pltpu.VMEM(output_grads.shape, BF16),
            pltpu.VMEM(probe_matrix.shape, BF16),
            *pieces,
            *pieces,
            *[pltpu.VMEM((k, tokens), BF16)] * 4,
            *columns,
            *columns,
            *[pltpu.VMEM((w, k), BF16) for w in (features, units, features)],
            pltpu.VMEM((2, 2, chunks, k, chunk), BF16),
            pltpu.VMEM((2, 2, chunks, k, chunk), BF16),
            pltpu.VMEM((2, chunks, k, chunk), BF16),
            pltpu.VMEM((tokens, k), F32),
            pltpu.VMEM((3, k, k), F32),
            pltpu.VMEM((3, n_mp, k // n_mp, k), F32),
            pltpu.VMEM((3, n_dp, k // n_mp, k), F32),
            pltpu.VMEM((3, k, k), F32),
            pltpu.VMEM((k, k), F32),
            pltpu.SemaphoreType.DMA((n_mp + 2,)),
            pltpu.SemaphoreType.DMA((4, 2, n_mp)),
            pltpu.SemaphoreType.DMA((4, 2, n_mp)),
            pltpu.SemaphoreType.DMA((4, 2, n_dp)),
            pltpu.SemaphoreType.DMA((4, 2, n_dp)),
            pltpu.SemaphoreType.DMA((3, 2, n_mp)),
            pltpu.SemaphoreType.DMA((3, 2, n_mp)),
            pltpu.SemaphoreType.DMA((3, n_dp)),
            pltpu.SemaphoreType.DMA((3, n_dp)),
            pltpu.SemaphoreType.DMA((2, 2, chunks)),
            pltpu.SemaphoreType.DMA((2, 2, chunks)),
            pltpu.SemaphoreType.DMA((2, 2, chunks)),
            pltpu.SemaphoreType.DMA((2, chunks)),
            pltpu.SemaphoreType.DMA((2, 2, chunks)),
        ],
        compiler_params=pltpu.CompilerParams(
            collective_id=0, has_side_effects=True, vmem_limit_bytes=56 * 2**20
        ),
    )(activations, output_grads, probe_matrix)
    return basis * jnp.sqrt(F32(H)), proj.astype(F32)


def contract_rows(left, right):
    return lax.dot_general(left, right, (((0,), (0,)), ((), ())), preferred_element_type=F32)


def token_total(partial_value):
    return lax.psum(partial_value.astype(BF16), "mp")


def orthonormalize(partial_value):
    summed = lax.psum(partial_value, "dp")
    gram = lax.dot_general(
        summed, summed, (((0,), (0,)), ((), ())),
        precision=lax.Precision.HIGHEST, preferred_element_type=F32,
    )
    factor = jnp.linalg.cholesky(lax.psum(gram, "mp"))
    return lax.linalg.triangular_solve(
        factor, summed, left_side=False, lower=True, transpose_a=True
    )


def separate(activations, output_grads, probe_matrix):
    def rows_of(field, columns):
        return token_total(jnp.dot(field, columns.astype(BF16), preferred_element_type=F32))

    first = orthonormalize(contract_rows(activations, rows_of(output_grads, probe_matrix)))
    second = orthonormalize(contract_rows(output_grads, rows_of(activations, first)))
    third = orthonormalize(contract_rows(activations, rows_of(output_grads, second)))
    projection = lax.psum(contract_rows(rows_of(activations, third), output_grads), "dp")
    return third * jnp.sqrt(F32(H)), projection


def solution(mesh):
    n_dp, n_mp = mesh.shape["dp"], mesh.shape["mp"]

    def on_device(activations, output_grads, probe_matrix):
        tokens, features = activations.shape
        units, k = probe_matrix.shape
        even = (
            n_dp == 4
            and n_mp % 2 == 0
            and features % (128 * n_dp) == 0
            and units % 512 == 0
            and tokens % (128 * n_mp) == 0
            and k % (8 * n_mp) == 0
            and k % 32 == 0
        )
        run = functools.partial(fused, n_dp, n_mp) if even else separate
        return run(activations, output_grads, probe_matrix)

    in_specs = (P("dp", "mp"), P("dp", "mp"), P("mp", None))
    out_specs = (P("mp", None), P(None, "mp"))
    return jax.shard_map(
        on_device, mesh=mesh, in_specs=in_specs, out_specs=out_specs, check_vma=False
    )
```

```python
import functools

import jax
import jax.numpy as jnp
from jax import lax
from jax.experimental import pallas as pl
from jax.experimental.pallas import tpu as pltpu
from jax.sharding import PartitionSpec as P

H = 8192
F32, BF16 = jnp.float32, jnp.bfloat16
MESH = pl.DeviceIdType.MESH


def inverse_factor(gram):
    k = gram.shape[0]
    lane_of = lax.broadcasted_iota(jnp.int32, (8, k), 1)
    m, e = gram, jnp.where(
        lax.broadcasted_iota(jnp.int32, (k, k), 0) == lax.broadcasted_iota(jnp.int32, (k, k), 1), 1.0, 0.0
    ).astype(F32)
    finished = []
    segment = k // 4

    def lane_at(x, lanes, j):
        return jnp.sum(jnp.where(lanes == j, x, 0.0), axis=1, keepdims=True)

    for first in range(0, k, segment):
        height = k - first
        lane_id = lax.broadcasted_iota(jnp.int32, (height, k), 1)
        row_id = first + lax.broadcasted_iota(jnp.int32, (height, k), 0)
        row_of = first + lax.broadcasted_iota(jnp.int32, (height, 1), 0)
        group_id = first // 8 + lax.broadcasted_iota(jnp.int32, (height // 8, 8, k), 0)

        def group_of(x, g, height=height, group_id=group_id):
            x = x.reshape(height // 8, 8, k)
            return jnp.sum(jnp.where(group_id == g, x, 0.0), axis=0)

        def step(g, carry, lane_id=lane_id, row_of=row_of, group_of=group_of):
            m, e = carry
            for half in (0, 4):
                m_rows, e_rows = group_of(m, g), group_of(e, g)
                at = [8 * g + half + p for p in range(4)]
                cols = [lane_at(m, lane_id, j) for j in at]
                small = [lane_at(m_rows, lane_of, j) for j in at]
                rows = [m_rows[half + p : half + p + 1, :] for p in range(4)]
                done = [e_rows[half + p : half + p + 1, :] for p in range(4)]
                for p in range(4):
                    inverse = 1.0 / small[p][half + p : half + p + 1, :]
                    for q in range(p + 1, 4):
                        ratio = small[p][half + q : half + q + 1, :] * inverse
                        rows[q] = rows[q] - ratio * rows[p]
                        done[q] = done[q] - ratio * done[p]
                        cols[q] = cols[q] - ratio * cols[p]
                        small[q] = small[q] - ratio * small[p]
                    scale = jnp.where(row_of > at[p], cols[p] * inverse, 0.0)
                    m = m - scale * rows[p]
                    e = e - scale * done[p]
            return m, e

        m, e = lax.fori_loop(first // 8, (first + segment) // 8, step, (m, e))
        top = jnp.where(lane_id == row_id, m, 0.0)[:segment]
        finished.append(e[:segment] * lax.rsqrt(jnp.sum(top, axis=1, keepdims=True)))
        m, e = m[segment:], e[segment:]
    return jnp.concatenate(finished, axis=0)


def kernel(
    n_dp, n_mp, acts, grads, probe, basis, proj,
    acts_v, grads_v, probe_v,
    part0, part1, part2, part3, came0, came1, came2, came3, rows0, rows1, rows2, rows3,
    sent0, sent2, got0, got2, sk0, sk1, sk2,
    up_part, up_came, cross_came,
    gram_part, gram_came, gram_sums, gram_all, factor,
    load_sem, mp_send, mp_recv, dp_send, dp_recv, g_send, g_recv, gd_send, gd_recv,
    out_send, in_send, up_recv, cross_recv, done_recv,
):
    me_d, me_m = lax.axis_index("dp"), lax.axis_index("mp")
    tokens, k = acts_v.shape[0], probe_v.shape[1]
    span = tokens // n_mp
    parts, cames = (part0, part1, part2, part3), (came0, came1, came2, came3)
    rows = (rows0, rows1, rows2, rows3)
    sents, gots = (sent0, None, sent2, None), (got0, None, got2, None)
    sketches = (sk0, sk1, sk2, proj)

    def span_of(c):
        return pl.ds(pl.multiple_of(c * span, span), span)

    def grads_load(c):
        return pltpu.make_async_copy(
            grads.at[span_of(c), :], grads_v.at[span_of(c), :], load_sem.at[c]
        )

    probe_load = pltpu.make_async_copy(probe, probe_v, load_sem.at[n_mp])
    acts_load = pltpu.make_async_copy(acts, acts_v, load_sem.at[n_mp + 1])
    probe_load.start()
    for i in range(n_mp):
        grads_load(lax.rem(me_m + 1 + i, n_mp)).start()
    acts_load.start()

    barrier = pltpu.get_barrier_semaphore()
    for i in range(1, n_mp):
        pl.semaphore_signal(
            barrier, inc=1, device_id={"mp": lax.rem(me_m + i, n_mp)}, device_id_type=MESH
        )
    for i in range(1, n_dp):
        pl.semaphore_signal(
            barrier, inc=1, device_id={"dp": lax.rem(me_d + i, n_dp)}, device_id_type=MESH
        )
    probe_load.wait()
    pl.semaphore_wait(barrier, n_mp + n_dp - 2)

    def copy(axis, src, dst, send, recv, peer):
        return pltpu.make_async_remote_copy(
            src_ref=src, dst_ref=dst, send_sem=send, recv_sem=recv,
            device_id={axis: peer}, device_id_type=MESH,
        )

    def gather_rows(s, piece, meanwhile=None):
        target = rows[s].at[:, span_of(me_m)]
        target[...] = piece.astype(BF16)

        pair = me_m + 1 - 2 * lax.rem(me_m, 2)
        peers = [lax.rem(me_m + i, n_mp) for i in range(2, n_mp, 2)] + [pair]

        def far(chunk, send, owner, peer):
            return copy("mp", chunk, chunk, mp_send.at[s, 1, send], mp_recv.at[s, 1, owner], peer)

        def twin(peer):
            return peer + 1 - 2 * lax.rem(peer, 2)

        for peer in peers:
            far(target, peer, me_m, peer).start()
        for peer in peers[:-1]:
            theirs = rows[s].at[:, span_of(peer)]
            far(theirs, peer, peer, peer).wait_recv()
            far(theirs, twin(peer), peer, pair).start()
        if meanwhile is not None:
            meanwhile()
        for peer in peers[:-1]:
            theirs = rows[s].at[:, span_of(twin(peer))]
            far(theirs, twin(peer), twin(peer), pair).wait()
            far(target, peer, me_m, peer).wait_send()
        far(rows[s].at[:, span_of(pair)], pair, pair, pair).wait()

    def scatter_rows(s, product, first, last):
        def body(i, _):
            c = lax.rem(me_m + i, n_mp)
            parts[s].at[c][...] = product(c).astype(BF16)

            @pl.when(i < n_mp)
            def _():
                copy(
                    "mp", parts[s].at[c], cames[s].at[me_m],
                    mp_send.at[s, 0, c], mp_recv.at[s, 0, me_m], c,
                ).start()

            return 0

        lax.fori_loop(first, last, body, 0)

    def collect_rows(s):
        def add(i, total):
            peer = lax.rem(me_m + i, n_mp)
            copy(
                "mp", parts[s].at[peer], cames[s].at[peer],
                mp_send.at[s, 0, peer], mp_recv.at[s, 0, peer], peer,
            ).wait()
            return total + cames[s].at[peer][...].astype(F32)

        return lax.fori_loop(1, n_mp, add, parts[s].at[me_m][...].astype(F32))

    def sum_tokens(s, field):
        width = field.shape[1] // n_dp

        def cols(j):
            return pl.ds(pl.multiple_of(j * width, 128), width)

        def body(i, _):
            j = lax.rem(me_d + i, n_dp)
            sents[s].at[j][...] = jnp.dot(
                rows[s][...], field[:, cols(j)], preferred_element_type=F32
            ).astype(BF16)

            @pl.when(i < n_dp)
            def _():
                copy(
                    "dp", sents[s].at[j], gots[s].at[me_d],
                    dp_send.at[s, 0, j], dp_recv.at[s, 0, me_d], j,
                ).start()

            return 0

        lax.fori_loop(1, n_dp + 1, body, 0)
        total = sents[s].at[me_d][...].astype(F32)
        for i in range(1, n_dp):
            peer = lax.rem(me_d + i, n_dp)
            copy(
                "dp", sents[s].at[peer], gots[s].at[peer],
                dp_send.at[s, 0, peer], dp_recv.at[s, 0, peer], peer,
            ).wait()
            total = total + gots[s].at[peer][...].astype(F32)
        share = total.astype(BF16)
        gram_part.at[s][...] = gram_of(share)
        gram_start(s)
        target = sketches[s].at[cols(me_d), :]
        target[...] = total.T.astype(BF16)
        for i in range(1, n_dp):
            peer = lax.rem(me_d + i, n_dp)
            copy("dp", target, target, dp_send.at[s, 1, peer], dp_recv.at[s, 1, me_d], peer).start()
        gram_across(s)
        gram_middle(s)
        for i in range(1, n_dp):
            peer = lax.rem(me_d + i, n_dp)
            theirs = sketches[s].at[cols(peer), :]
            copy("dp", target, theirs, dp_send.at[s, 1, peer], dp_recv.at[s, 1, peer], peer).wait()

    def sum_tokens_line(w, s, field):
        chunks, width = cross_came.shape[1], cross_came.shape[3]
        edge = (me_d == 0) | (me_d == n_dp - 1)
        inner = 1 + me_d // 3
        other, outer = 3 - me_d, 3 * (me_d - 1)

        def cols(half, t):
            return pl.ds(pl.multiple_of((half * chunks + t) * width, width), width)

        def product(half, t):
            return jnp.dot(rows[s][...], field[:, cols(half, t)], preferred_element_type=F32)

        def up(half, t, peer):
            return copy(
                "dp", up_part.at[w, half, t], up_came.at[w, half, t],
                out_send.at[w, half, t], up_recv.at[w, half, t], peer,
            )

        def cross(half, t):
            return copy(
                "dp", up_part.at[w, half, t], cross_came.at[w, t],
                in_send.at[w, 0, t], cross_recv.at[w, t], other,
            )

        def done(half, t, send, peer):
            if s == 3:
                chunk = sketches[s].at[:, cols(half, t)]
            else:
                chunk = sketches[s].at[cols(half, t), :]
            return copy("dp", chunk, chunk, send, done_recv.at[w, half, t], peer)

        if s != 3:
            gram_part.at[s][...] = jnp.zeros((k, k), F32)

        @pl.when(edge)
        def _():
            near, far = inner - 1, 2 - inner

            def give(half, t):
                up_part.at[w, half, t][...] = product(half, t).astype(BF16)
                up(half, t, inner).start()

            def take(half, t):
                up(half, t, inner).wait_send()
                done(half, t, out_send.at[w, half, t], inner).wait_recv()

            def body(t, _):
                @pl.when(t < chunks)
                def _():
                    give(far, t)

                @pl.when((t >= 1) & (t < chunks + 1))
                def _():
                    give(near, t - 1)

                @pl.when((t >= 3) & (t < chunks + 3))
                def _():
                    take(near, t - 3)

                @pl.when(t >= 4)
                def _():
                    take(far, t - 4)

                return 0

            lax.fori_loop(0, chunks + 4, body, 0)

        @pl.when(jnp.logical_not(edge))
        def _():
            mine, theirs = me_d - 1, 2 - me_d

            def body(t, _):
                @pl.when(t < chunks)
                def _():
                    total = product(theirs, t)
                    up(theirs, t, outer).wait_recv()
                    total = total + up_came.at[w, theirs, t][...].astype(F32)
                    up_part.at[w, theirs, t][...] = total.astype(BF16)
                    cross(theirs, t).start()

                @pl.when((t >= 1) & (t < chunks + 1))
                def _():
                    u = t - 1
                    total = product(mine, u)
                    up(mine, u, outer).wait_recv()
                    cross(mine, u).wait_recv()
                    total = total + up_came.at[w, mine, u][...].astype(F32)
                    total = total + cross_came.at[w, u][...].astype(F32)
                    if s == 3:
                        sketches[s].at[:, cols(mine, u)][...] = total.astype(BF16)
                    else:
                        sketches[s].at[cols(mine, u), :][...] = total.T.astype(BF16)
                    done(mine, u, out_send.at[w, 1, u], other).start()
                    done(mine, u, out_send.at[w, 0, u], outer).start()
                    if s != 3:
                        gram_part.at[s][...] += gram_of(total.astype(BF16))

                @pl.when(t >= 2)
                def _():
                    u = t - 2
                    done(theirs, u, in_send.at[w, 1, u], other).wait_recv()
                    done(theirs, u, in_send.at[w, 1, u], outer).start()

                return 0

            def end(t, _):
                cross(theirs, t).wait_send()
                done(mine, t, out_send.at[w, 1, t], other).wait_send()
                done(mine, t, out_send.at[w, 0, t], outer).wait_send()
                done(theirs, t, in_send.at[w, 1, t], outer).wait_send()
                return 0

            lax.fori_loop(0, chunks + 2, body, 0)
            lax.fori_loop(0, chunks, end, 0)

    g_rows = k // n_mp

    def g_span(c):
        return pl.ds(pl.multiple_of(c * g_rows, g_rows), g_rows)

    def gram_of(share):
        return lax.dot_general(
            share, share, (((1,), (1,)), ((), ())), preferred_element_type=F32
        )

    def gram_start(s):
        gram_came.at[s, me_m][...] = gram_part.at[s, g_span(me_m), :][...]
        for i in range(1, n_mp):
            peer = lax.rem(me_m + i, n_mp)
            copy(
                "mp", gram_part.at[s, g_span(peer), :], gram_came.at[s, me_m],
                g_send.at[s, 0, peer], g_recv.at[s, 0, me_m], peer,
            ).start()

    def gram_across(s):
        for i in range(1, n_mp):
            peer = lax.rem(me_m + i, n_mp)
            copy(
                "mp", gram_part.at[s, g_span(peer), :], gram_came.at[s, peer],
                g_send.at[s, 0, peer], g_recv.at[s, 0, peer], peer,
            ).wait()
        total = gram_came.at[s, 0][...]
        for i in range(1, n_mp):
            total = total + gram_came.at[s, i][...]
        target = gram_sums.at[s, me_d]
        target[...] = total
        for i in range(1, n_dp):
            peer = lax.rem(me_d + i, n_dp)
            copy("dp", target, target, gd_send.at[s, peer], gd_recv.at[s, me_d], peer).start()

    def gram_middle(s):
        for i in range(1, n_dp):
            peer = lax.rem(me_d + i, n_dp)
            theirs = gram_sums.at[s, peer]
            copy("dp", gram_sums.at[s, me_d], theirs, gd_send.at[s, peer], gd_recv.at[s, peer], peer).wait()
        target = gram_all.at[s, g_span(me_m), :]
        total = gram_sums.at[s, 0][...]
        for i in range(1, n_dp):
            total = total + gram_sums.at[s, i][...]
        target[...] = total
        for i in range(1, n_mp):
            peer = lax.rem(me_m + i, n_mp)
            copy("mp", target, target, g_send.at[s, 1, peer], g_recv.at[s, 1, me_m], peer).start()

    def gram_end(s):
        target = gram_all.at[s, g_span(me_m), :]
        for i in range(1, n_mp):
            peer = lax.rem(me_m + i, n_mp)
            theirs = gram_all.at[s, g_span(peer), :]
            copy("mp", target, theirs, g_send.at[s, 1, peer], g_recv.at[s, 1, peer], peer).wait()
        factor[...] = inverse_factor(gram_all.at[s][...])

    def probe_product(c):
        grads_load(c).wait()
        return jnp.dot(grads_v[span_of(c), :], probe_v[...], preferred_element_type=F32)

    scatter_rows(0, probe_product, 1, n_mp + 1)
    gather_rows(0, collect_rows(0).T)
    acts_load.wait()

    def write_basis():
        basis[...] = lax.dot_general(
            sk2[...].astype(F32), factor[...], (((1,), (1,)), ((), ())),
            precision=lax.Precision.HIGHEST, preferred_element_type=F32,
        )

    for s, (field, into) in enumerate(((acts_v, acts_v), (grads_v, grads_v), (acts_v, acts_v))):
        if s == 1:
            sum_tokens_line(0, s, field)
            gram_start(s)
        else:
            sum_tokens(s, field)

        def product(c, s=s, into=into):
            return jnp.dot(
                into[span_of(c), :], sketches[s][...], preferred_element_type=F32
            )

        if s == 1:
            third = n_mp // 3 + 1
            scatter_rows(s + 1, product, 1, third)
            gram_across(s)
            scatter_rows(s + 1, product, third, 2 * third - 1)
            gram_middle(s)
            scatter_rows(s + 1, product, 2 * third - 1, n_mp + 1)
        else:
            scatter_rows(s + 1, product, 1, n_mp + 1)
        gram_end(s)
        total = collect_rows(s + 1)
        gather_rows(
            s + 1,
            lax.dot_general(
                factor[...], total, (((1,), (1,)), ((), ())),
                precision=lax.Precision.HIGHEST, preferred_element_type=F32,
            ),
            write_basis if s == 2 else None,
        )
    sum_tokens_line(1, 3, grads_v)


def fused(n_dp, n_mp, activations, output_grads, probe_matrix):
    tokens, features = activations.shape
    units, k = probe_matrix.shape
    span = tokens // n_mp
    chunk, chunks = 256, units // 512
    any_space = pl.BlockSpec(memory_space=pl.ANY)
    vmem = pl.BlockSpec(memory_space=pltpu.VMEM)
    pieces = [pltpu.VMEM((n_mp, span, k), BF16)] * 4
    columns = [pltpu.VMEM((n_dp, k, features // n_dp), BF16)] * 2
    basis, proj = pl.pallas_call(
        functools.partial(kernel, n_dp, n_mp),
        out_shape=(
            jax.ShapeDtypeStruct((features, k), F32),
            jax.ShapeDtypeStruct((k, units), BF16),
        ),
        in_specs=[any_space] * 3,
        out_specs=(vmem, vmem),
        scratch_shapes=[
            pltpu.VMEM(activations.shape, BF16),
            pltpu.VMEM(output_grads.shape, BF16),
            pltpu.VMEM(probe_matrix.shape, BF16),
            *pieces,
            *pieces,
            *[pltpu.VMEM((k, tokens), BF16)] * 4,
            *columns,
            *columns,
            *[pltpu.VMEM((w, k), BF16) for w in (features, units, features)],
            pltpu.VMEM((2, 2, chunks, k, chunk), BF16),
            pltpu.VMEM((2, 2, chunks, k, chunk), BF16),
            pltpu.VMEM((2, chunks, k, chunk), BF16),
            pltpu.VMEM((3, k, k), F32),
            pltpu.VMEM((3, n_mp, k // n_mp, k), F32),
            pltpu.VMEM((3, n_dp, k // n_mp, k), F32),
            pltpu.VMEM((3, k, k), F32),
            pltpu.VMEM((k, k), F32),
            pltpu.SemaphoreType.DMA((n_mp + 2,)),
            pltpu.SemaphoreType.DMA((4, 2, n_mp)),
            pltpu.SemaphoreType.DMA((4, 2, n_mp)),
            pltpu.SemaphoreType.DMA((4, 2, n_dp)),
            pltpu.SemaphoreType.DMA((4, 2, n_dp)),
            pltpu.SemaphoreType.DMA((3, 2, n_mp)),
            pltpu.SemaphoreType.DMA((3, 2, n_mp)),
            pltpu.SemaphoreType.DMA((3, n_dp)),
            pltpu.SemaphoreType.DMA((3, n_dp)),
            pltpu.SemaphoreType.DMA((2, 2, chunks)),
            pltpu.SemaphoreType.DMA((2, 2, chunks)),
            pltpu.SemaphoreType.DMA((2, 2, chunks)),
            pltpu.SemaphoreType.DMA((2, chunks)),
            pltpu.SemaphoreType.DMA((2, 2, chunks)),
        ],
        compiler_params=pltpu.CompilerParams(
            collective_id=0, has_side_effects=True, vmem_limit_bytes=56 * 2**20
        ),
    )(activations, output_grads, probe_matrix)
    return basis * jnp.sqrt(F32(H)), proj.astype(F32)


def contract_rows(left, right):
    return lax.dot_general(left, right, (((0,), (0,)), ((), ())), preferred_element_type=F32)


def token_total(partial_value):
    return lax.psum(partial_value.astype(BF16), "mp")


def orthonormalize(partial_value):
    summed = lax.psum(partial_value, "dp")
    gram = lax.dot_general(
        summed, summed, (((0,), (0,)), ((), ())),
        precision=lax.Precision.HIGHEST, preferred_element_type=F32,
    )
    factor = jnp.linalg.cholesky(lax.psum(gram, "mp"))
    return lax.linalg.triangular_solve(
        factor, summed, left_side=False, lower=True, transpose_a=True
    )


def separate(activations, output_grads, probe_matrix):
    def rows_of(field, columns):
        return token_total(jnp.dot(field, columns.astype(BF16), preferred_element_type=F32))

    first = orthonormalize(contract_rows(activations, rows_of(output_grads, probe_matrix)))
    second = orthonormalize(contract_rows(output_grads, rows_of(activations, first)))
    third = orthonormalize(contract_rows(activations, rows_of(output_grads, second)))
    projection = lax.psum(contract_rows(rows_of(activations, third), output_grads), "dp")
    return third * jnp.sqrt(F32(H)), projection


def solution(mesh):
    n_dp, n_mp = mesh.shape["dp"], mesh.shape["mp"]

    def on_device(activations, output_grads, probe_matrix):
        tokens, features = activations.shape
        units, k = probe_matrix.shape
        even = (
            n_dp == 4
            and n_mp % 2 == 0
            and features % (128 * n_dp) == 0
            and units % 512 == 0
            and tokens % (128 * n_mp) == 0
            and k % (8 * n_mp) == 0
            and k % 32 == 0
        )
        run = functools.partial(fused, n_dp, n_mp) if even else separate
        return run(activations, output_grads, probe_matrix)

    in_specs = (P("dp", "mp"), P("dp", "mp"), P("mp", None))
    out_specs = (P("mp", None), P(None, "mp"))
    return jax.shard_map(
        on_device, mesh=mesh, in_specs=in_specs, out_specs=out_specs, check_vma=False
    )
```
